32 devices in a mesh: slab: 2 (over x), xy: 8 (over z, y), gz: 2 (over core).
Axes of the slice: x: 2, y: 2, z: 4, core: 2. Of those that a mesh axis runs over, the one named last changes fastest.
Arguments:
- source_rows: bfloat16 [32768, 128], P(('slab', 'xy', 'gz')), parts along dimension 0, may hold values from 0 to 1
- interp_bank: bfloat16 [2, 16, 128, 256], replicated, may hold values from -0.375 to 0.375
- source_taps: int32 [2, 65536], P(None, ('slab', 'xy', 'gz')), parts along dimension 1, may hold values from 0 to 1023
- tap_phase: int32 [2, 65536], P(None, ('slab', 'xy', 'gz')), parts along dimension 1, may hold values from 0 to 15
- mesh_node: int32 [65536], P(('slab', 'xy', 'gz')), parts along dimension 0, may hold values from 0 to 127
- target_tile: int32 [65536, 1], P(('slab', 'xy', 'gz')), parts along dimension 0, may hold values from 0 to 15; in each aligned block of 2048 rows (0 to 2047, 2048 to 4095, ...) at most 256 rows name the same one
- target_row: int32 [65536], P(('slab', 'xy', 'gz')), parts along dimension 0, may hold values from 0 to 1023
- tile_owner: int32 [32], P('slab'), parts along dimension 0, may hold values from 0 to 15, each once
- coarse_mesh: float32 [4, 2, 128], P(('slab', 'gz'), None, 'xy'), parts along dimension 0, may hold values from 0 to 1
Outputs:
- blended: bfloat16 [32768, 128], P(('slab', 'xy', 'gz')), parts along dimension 0
The draws below stay inside these ranges and needn't reach their ends.
There are 2 independent parts, one for each index of `slab`. The reference program is written for one: setup_inputs(seed, part) draws one part's arguments, and reference() takes and returns one part's arrays. A program takes and returns all parts, laid end to end along the dimension named above; an argument that names none is the same for every part. Nothing has to cross between parts.
Inputs may be any that keep to these rules, and one draw needn't show every extreme that they name: `target_tile`: among the 2048 contributions of one device, at most 256 intersect any one output tile, and some tile is intersected by exactly 256 of them. `tile_owner`: each device index owns exactly one output tile.
All inputs are finite; a program needn't handle non-finite values.
Results may differ from the reference program's by a relative error of at most 0.0057.
Values may be sent and summed in bfloat16 or wider, within the bound.
A program may use at most 64 MiB of HBM per device.

```python
import math
import jax
import jax.numpy as jnp
import numpy as np
from jax import lax

VOXELS = 128
TAPS = 2
PHASES = 16
CONTRIB = 2048
OWNERS = 16
SOURCE_DEV = 1024
TILE_ROWS = 1024
CAPACITY = 256
MESH = 128
SPREAD = 32
N_XY = 8
N_GZ = 2


def touch_ends(array, rng, least, top_value):
    place = [jax.random.randint(jax.random.fold_in(rng, axis), (), 0, length) for axis, length in enumerate(array.shape)]
    main_axis = array.shape.index(max(array.shape))
    next_to = place[:main_axis] + [(place[main_axis] + 1) % array.shape[main_axis]] + place[main_axis + 1:]
    return array.at[tuple(place)].set(least).at[tuple(next_to)].set(top_value)


def level_of(key, extent, cuts, smallest, top_value):
    factor_of = 1.0
    for dim, blocks in cuts:
        heights = jax.random.uniform(jax.random.fold_in(jax.random.fold_in(key, 6), dim), (blocks,), jnp.float32, smallest / len(cuts), top_value / len(cuts))
        factor_of = factor_of * jnp.repeat(jnp.exp(heights), extent[dim] // blocks).reshape((-1,) + (1,) * (len(extent) - 1 - dim))
    return factor_of


def routed_block(rng, own, number, rows, count, top, reach, slope):
    order = jax.random.permutation(rng, count)
    crowded, ordinary = load_shares(count, rows * top, reach, slope, True), load_shares(count, rows * top, reach, slope, False)
    places = jnp.arange(count)

    def named(sizes, offset_by):
        used = int((sizes > 0).sum())
        fixed = max(1, used // 4)
        shifted = fixed + (places - fixed + offset_by * (used - fixed)) % max(1, count - fixed)
        return jnp.zeros((count,), jnp.int32).at[order[jnp.where(places < fixed, places, shifted)]].set(jnp.asarray(sizes, jnp.int32))

    sizes = jnp.where(number % 4 == 0, named(crowded, number // 4), named(ordinary, number - number // 4 - 1))
    mixed = jax.random.permutation(jax.random.fold_in(own, 3), count)
    giver, receiver = mixed[0:count // 2 * 2:2], mixed[1:count // 2 * 2:2]
    room = jnp.minimum(sizes[giver] - 1, reach - sizes[receiver]) // 2
    room = jnp.where((giver == order[0]) | (receiver == order[0]) | (sizes[receiver] == 0), 0, jnp.maximum(room, 0))
    shifted = jax.random.randint(jax.random.fold_in(own, 4), (count // 2,), 0, 1 << 20) % (room + 1)
    sizes = sizes.at[giver].add(-shifted).at[receiver].add(shifted)
    labels = jnp.searchsorted(jnp.cumsum(sizes), jnp.arange(rows * top), side="right").astype(jnp.int32)
    table = labels.reshape(top, rows).T
    table = table[jax.random.permutation(jax.random.fold_in(own, 1), rows)]
    offset_by = jax.random.randint(jax.random.fold_in(own, 2), (rows, 1), 0, top)
    return jnp.take_along_axis(table, (jnp.arange(top)[None, :] + offset_by) % top, axis=1)


def load_shares(count, total, most, skew, full):
    weights = [(1 << 20) // math.isqrt(standing ** skew) + 1 for standing in range(1, count + 1)]
    largest = most if full else min(most, max(-(-total // count), total * weights[0] // sum(weights)))
    least = 1 if total - largest >= count - 1 else 0
    counts, rest = [largest] + [least] * (count - 1), total - largest - least * (count - 1)
    while rest > 0:
        candidates = [i for i in range(1, count) if counts[i] < largest] or [i for i in range(1, count) if counts[i] < most]
        mass, budget = sum([weights[i] for i in candidates]), rest
        for i in candidates:
            addition = min(most - counts[i], max(1, budget * weights[i] // mass), rest)
            counts[i] = counts[i] + addition
            rest = rest - addition
    return np.array(counts)


def gaussian(rng, extent, scale, limit, kind=jnp.bfloat16):
    entries = scale * jax.random.normal(rng, extent, jnp.float32)
    return jnp.clip(entries, min=-limit, max=limit).astype(kind)


def setup_inputs(seed: int = 0, part: int = 0) -> dict:
    keys = jax.random.split(jax.random.key(seed), 10)
    part_splits = jax.random.split(jax.random.fold_in(keys[9], part), 10)
    source_rows = jnp.clip(1.0 * jax.random.uniform(part_splits[0], (OWNERS * SOURCE_DEV, VOXELS), jnp.float32) ** level_of(part_splits[0], (OWNERS * SOURCE_DEV, VOXELS), ((0, 16),), -0.2, 0.2), 0.0, 1.0).astype(jnp.bfloat16)
    interp_bank = gaussian(keys[1], (TAPS, PHASES, VOXELS, 2 * VOXELS), (TAPS * VOXELS) ** -0.5, 0.375)
    source_taps = touch_ends(jax.random.randint(part_splits[2], (TAPS, OWNERS * CONTRIB), 0, SOURCE_DEV), jax.random.fold_in(part_splits[2], 1), 0, SOURCE_DEV - 1).astype(jnp.int32)
    tap_phase = touch_ends(jax.random.randint(part_splits[3], (TAPS, OWNERS * CONTRIB), 0, PHASES), jax.random.fold_in(part_splits[3], 1), 0, PHASES - 1).astype(jnp.int32)
    mesh_node = touch_ends(jax.random.randint(part_splits[4], (OWNERS * CONTRIB,), 0, MESH), jax.random.fold_in(part_splits[4], 1), 0, MESH - 1).astype(jnp.int32)
    target_tile_keys = jax.random.split(jax.random.fold_in(part_splits[5], 1), (OWNERS * CONTRIB) // CONTRIB)
    target_tile_turns = jax.random.permutation(jax.random.fold_in(part_splits[5], 3), (OWNERS * CONTRIB) // CONTRIB)
    target_tile = jax.vmap(lambda own, number: routed_block(jax.random.fold_in(part_splits[5], 2), own, number, CONTRIB, OWNERS, 1, CAPACITY, 2))(target_tile_keys, target_tile_turns).reshape((OWNERS * CONTRIB, 1))
    target_row = touch_ends(jax.random.randint(part_splits[6], (OWNERS * CONTRIB,), 0, TILE_ROWS), jax.random.fold_in(part_splits[6], 1), 0, TILE_ROWS - 1).astype(jnp.int32)
    tile_owner = jax.random.permutation(part_splits[7], OWNERS).astype(jnp.int32)
    coarse_mesh = jnp.clip(1.0 * jax.random.uniform(part_splits[8], (N_GZ, 2, MESH), jnp.float32) ** level_of(part_splits[8], (N_GZ, 2, MESH), ((0, 2), (2, 8)), -0.2, 0.2), 0.0, 1.0)
    return dict(source_rows=source_rows, interp_bank=interp_bank, source_taps=source_taps, tap_phase=tap_phase, mesh_node=mesh_node, target_tile=target_tile, target_row=target_row, tile_owner=tile_owner, coarse_mesh=coarse_mesh)


floor_weight = 0.1


def reference(source_rows, interp_bank, source_taps, tap_phase, mesh_node, target_tile, target_row, tile_owner, coarse_mesh):
    owners = N_XY * N_GZ
    sources = source_rows.reshape(owners, SOURCE_DEV, VOXELS)
    taps_all = source_taps.reshape(TAPS, owners, CONTRIB).transpose(1, 0, 2)
    phase_all = tap_phase.reshape(TAPS, owners, CONTRIB).transpose(1, 0, 2)
    nodes_all = mesh_node.reshape(owners, CONTRIB)
    groups = (jnp.arange(owners, dtype=jnp.int32) % N_GZ).astype(jnp.int32)
    widened = interp_bank.transpose(0, 2, 1, 3).reshape(TAPS, VOXELS, PHASES * 2 * VOXELS)
    phase_ids = jnp.arange(PHASES, dtype=jnp.int32)

    def one_device(inputs):
        rows, taps_here, phase_here, nodes_here, group = inputs
        mesh_here = coarse_mesh[group]
        shift = mesh_here[0][nodes_here]
        center = ((VOXELS - 1) * mesh_here[1][nodes_here]).astype(jnp.bfloat16)
        total = jnp.zeros((CONTRIB, 2 * VOXELS), jnp.float32)
        for tap_index in range(TAPS):
            picked = rows[taps_here[tap_index]]
            product = jnp.dot(picked, widened[tap_index], preferred_element_type=jnp.float32)
            product = product.reshape(CONTRIB, PHASES, 2 * VOXELS)
            selector = (phase_here[tap_index][:, None] == phase_ids[None, :]).astype(jnp.float32)
            total = total + jnp.sum(product * selector[:, :, None], axis=1)
        weight = shift[:, None]
        mixed = ((1.0 - weight) * total[:, :VOXELS] + weight * total[:, VOXELS:]).astype(jnp.bfloat16)
        return mixed, center

    mixed, center = lax.map(one_device, (sources, taps_all, phase_all, nodes_all, groups))
    mixed = lax.optimization_barrier(mixed)
    values = mixed.reshape(owners * CONTRIB, VOXELS).astype(jnp.float32)
    centers = center.reshape(owners * CONTRIB).astype(jnp.float32)
    offsets = jnp.arange(VOXELS, dtype=jnp.float32)[None, :] - centers[:, None]
    weights = jnp.exp(-0.5 * (offsets / SPREAD) ** 2)
    index = (target_tile[:, 0] * TILE_ROWS + target_row).astype(jnp.int32)
    weighted_sum = jax.ops.segment_sum(weights * values, index, num_segments=owners * TILE_ROWS)
    weight_sum = jax.ops.segment_sum(weights, index, num_segments=owners * TILE_ROWS)
    tiles = (weighted_sum / jnp.maximum(weight_sum, floor_weight)).reshape(owners, TILE_ROWS, VOXELS)
    placed = jnp.zeros_like(tiles).at[tile_owner].set(tiles)
    return placed.reshape(owners * TILE_ROWS, VOXELS).astype(jnp.bfloat16)
```

```python
import functools

import jax
import jax.numpy as jnp
from jax import lax
from jax.experimental import pallas as pl
from jax.experimental.pallas import tpu as pltpu
from jax.sharding import PartitionSpec as P

floor_weight = 0.1
LANES = 128
INFO = 16
MESH_ROW = 6
META = 16
f32, bf16, i32 = jnp.float32, jnp.bfloat16, jnp.int32
NT = (((1,), (1,)), ((), ()))


def flip(a, b, count):
    out, bit = 0, 1
    while bit < count:
        out = out + ((a // bit + b // bit) % 2) * bit
        bit *= 2
    return out


def one_hot(columns, values):
    return jnp.where(columns == values, 1.0, 0.0).astype(bf16)


def kernel(
    sizes,
    source_ref, bank_hbm, taps_ref, phase_ref, node_ref, tile_ref, row_ref, owner_ref, mesh_ref,
    out_ref,
    bank, member, info_rows, info_all, placed, acc, mesh_own, mesh_got, sent, got,
    bank_sem, mesh_send, mesh_recv, send_sem, recv_sem,
):
    contrib, owners, plane, group, cap, wide, nodes = sizes
    voxels = source_ref.shape[1]
    rows_src = source_ref.shape[0]
    tile_rows = out_ref.shape[0]
    phases = placed.shape[1] // (2 * voxels)
    spread = float(voxels // 4)
    slab_at, xy_at, gz_at = lax.axis_index("slab"), lax.axis_index("xy"), lax.axis_index("gz")
    me = xy_at * group + gz_at

    def device(step):
        other = flip(me, step, owners)
        return (slab_at, other // group, other % group)

    barrier = pltpu.get_barrier_semaphore()

    @pl.loop(1, owners)
    def _(step):
        pl.semaphore_signal(barrier, inc=1, device_id=device(step), device_id_type=pl.DeviceIdType.MESH)

    bank_copy = pltpu.make_async_copy(bank_hbm, bank, bank_sem)
    bank_copy.start()

    part = mesh_ref.shape[2]
    place = jnp.where(
        lax.broadcasted_iota(i32, (part, nodes), 1) == lax.broadcasted_iota(i32, (part, nodes), 0) + xy_at * part, 1.0, 0.0
    )
    mesh_own[...] = jnp.dot(mesh_ref[0], place, precision=lax.Precision.HIGHEST, preferred_element_type=f32)

    pl.semaphore_wait(barrier, owners - 1)

    def mesh_copy(step):
        return pltpu.make_async_remote_copy(
            src_ref=mesh_own,
            dst_ref=mesh_got.at[step],
            send_sem=mesh_send.at[step],
            recv_sem=mesh_recv.at[step],
            device_id=(slab_at, flip(xy_at, step, plane), gz_at),
            device_id_type=pl.DeviceIdType.MESH,
        )

    @pl.loop(1, plane)
    def _(step):
        mesh_copy(step).start()

    tiles = tile_ref[...]
    owner = jnp.zeros_like(tiles)
    for tile in range(owners):
        owner = jnp.where(tiles == tile, owner_ref[tile], owner)
    relative = jnp.bitwise_xor(owner, me)
    chosen = jnp.where(lax.broadcasted_iota(i32, (owners, contrib), 0) == relative, 1.0, 0.0)
    member[...] = chosen
    chunk = 256
    before = (
        lax.broadcasted_iota(i32, (chunk, chunk), 0) < lax.broadcasted_iota(i32, (chunk, chunk), 1)
    ).astype(f32).astype(bf16)
    carry = jnp.zeros((owners, 1), f32)
    ranks = []
    for at in range(0, contrib, chunk):
        here = chosen[:, at : at + chunk]
        earlier = jnp.dot(here.astype(bf16), before, preferred_element_type=f32) + carry
        ranks.append(jnp.sum(here * earlier, axis=0, keepdims=True))
        carry = carry + jnp.sum(here, axis=1, keepdims=True)
    rank = jnp.concatenate(ranks, axis=1)
    rank_hot = one_hot(lax.broadcasted_iota(i32, (wide, contrib), 0).astype(f32), rank)
    node_hot = one_hot(lax.broadcasted_iota(i32, (nodes, contrib), 0), node_ref[...])

    @pl.loop(1, plane)
    def _(step):
        mesh_copy(step).wait_recv()

    mesh = mesh_own[...]
    for step in range(1, plane):
        mesh = mesh + mesh_got[step]
    shift, center = mesh[0:1], (voxels - 1) * mesh[1:2]
    high = shift.astype(bf16).astype(f32)
    middle = (shift - high).astype(bf16).astype(f32)
    low = shift - high - middle
    spot = lax.broadcasted_iota(i32, (INFO, nodes), 0)
    table = jnp.zeros((INFO, nodes), f32)
    for at, line in enumerate((high, middle, low, center)):
        table = jnp.where(spot == MESH_ROW + at, line, table)
    info = jnp.dot(table.astype(bf16), node_hot, preferred_element_type=f32)
    target = row_ref[...] + 1
    taps0, taps1 = taps_ref[0:1, :], taps_ref[1:2, :]
    lines = {
        0: taps0 // 256, 1: taps0 % 256, 2: taps1 // 256, 3: taps1 % 256,
        4: phase_ref[0:1, :], 5: phase_ref[1:2, :],
        10: target // 256, 11: target % 256,
    }
    spot = lax.broadcasted_iota(i32, (INFO, contrib), 0)
    for at, line in lines.items():
        info = jnp.where(spot == at, line.astype(f32), info)

    @pl.loop(0, owners)
    def _(step):
        info_rows[pl.ds(pl.multiple_of(step * INFO, INFO), INFO), :] = (
            info * member[pl.ds(step, 1), :]
        ).astype(bf16)

    info_all[...] = lax.dot_general(info_rows[...], rank_hot, NT, preferred_element_type=f32)
    acc[...] = jnp.zeros_like(acc)
    bank_copy.wait()

    def value_copy(step):
        return pltpu.make_async_remote_copy(
            src_ref=sent.at[step],
            dst_ref=got.at[step],
            send_sem=send_sem.at[step],
            recv_sem=recv_sem.at[step],
            device_id=device(step),
            device_id_type=pl.DeviceIdType.MESH,
        )

    bundle = max(1, 256 // cap)
    size = bundle * cap
    lines_each = wide // LANES

    def produce(first):
        pieces = []
        for d in range(bundle):
            lanes = info_all[pl.ds(pl.multiple_of((first + d) * INFO, INFO), INFO), :]
            pieces.append(lanes.T[:cap])
            meta = [lanes[r : r + 1, at * LANES : (at + 1) * LANES] for r in (9, 10, 11) for at in range(lines_each)]
            spot = lax.broadcasted_iota(i32, (META, LANES), 0)
            filled = jnp.zeros((META, LANES), f32)
            for at, line in enumerate(meta):
                filled = jnp.where(spot == at, line, filled)
            sent[first + d, cap : cap + META, :] = filled.astype(bf16)
        columns = pieces[0] if bundle == 1 else jnp.concatenate(pieces, axis=0)
        source = source_ref[...]
        ids = lax.broadcasted_iota(i32, (size, rows_src), 1).astype(f32)
        for k in range(2):
            tap = columns[:, 2 * k : 2 * k + 1] * 256.0 + columns[:, 2 * k + 1 : 2 * k + 2]
            picked = jnp.dot(one_hot(ids, tap), source, preferred_element_type=f32).astype(bf16)
            phase = jnp.broadcast_to(columns[:, 4 + k : 5 + k], (size, voxels)).astype(bf16)
            for p in range(phases):
                at = (k * phases + p) * voxels
                placed[:, at : at + voxels] = jnp.where(phase == jnp.bfloat16(p), picked, jnp.bfloat16(0))
        products = jnp.dot(placed[...], bank[...], preferred_element_type=f32)
        weight = columns[:, MESH_ROW : MESH_ROW + 1] + columns[:, MESH_ROW + 1 : MESH_ROW + 2]
        weight = weight + columns[:, MESH_ROW + 2 : MESH_ROW + 3]
        mixed = ((1.0 - weight) * products[:, :voxels] + weight * products[:, voxels:]).astype(bf16)
        for d in range(bundle):
            sent[first + d, :cap, :] = mixed[d * cap : (d + 1) * cap]

            @pl.when(first + d > 0)
            def _():
                value_copy(first + d).start()

    def consume(values, meta):
        meta = meta.astype(f32)
        target = meta[lines_each : 2 * lines_each] * 256.0 + meta[2 * lines_each : 3 * lines_each]
        target = jnp.concatenate([target[at : at + 1] for at in range(lines_each)], axis=1)[:, :cap]
        turned = meta.T
        center = jnp.concatenate([turned[:, at : at + 1] for at in range(lines_each)], axis=0)[:cap]
        offsets = lax.broadcasted_iota(i32, (cap, voxels), 1).astype(f32) - center
        weights = jnp.exp(-0.5 * (offsets / spread) ** 2)
        operand = jnp.concatenate([weights * values.astype(f32), weights], axis=1).astype(bf16)
        ids = lax.broadcasted_iota(i32, (tile_rows, cap), 0).astype(f32) + 1.0
        acc[...] += jnp.dot(one_hot(ids, target), operand, preferred_element_type=f32)

    blocks = owners // bundle

    @pl.loop(0, blocks)
    def _(turn):
        produce((blocks - 1 - turn) * bundle)

    consume(sent[0, :cap, :], sent[0, cap : cap + META, :])

    @pl.loop(1, owners)
    def _(turn):
        step = owners - turn
        value_copy(step).wait_recv()
        consume(got[step, :cap, :], got[step, cap : cap + META, :])

    out_ref[...] = (acc[:, :voxels] / jnp.maximum(acc[:, voxels:], floor_weight)).astype(bf16)

    @pl.loop(1, plane)
    def _(step):
        mesh_copy(step).wait_send()

    @pl.loop(1, owners)
    def _(step):
        value_copy(step).wait_send()


def on_device(
    source_rows,
    interp_bank,
    source_taps,
    tap_phase,
    mesh_node,
    target_tile,
    target_row,
    tile_owner,
    coarse_mesh,
):
    contrib = mesh_node.shape[0]
    voxels = source_rows.shape[1]
    taps, phases = interp_bank.shape[:2]
    plane = lax.axis_size("xy")
    group = lax.axis_size("gz")
    owners = plane * group
    cap = 2 * contrib // owners
    wide = max(cap, LANES)
    tile_rows = contrib // 2
    nodes = plane * coarse_mesh.shape[2]
    bundle = max(1, 256 // cap)
    vmem = pl.BlockSpec(memory_space=pltpu.VMEM)
    return pl.pallas_call(
        functools.partial(kernel, (contrib, owners, plane, group, cap, wide, nodes)),
        out_shape=jax.ShapeDtypeStruct((tile_rows, voxels), bf16),
        in_specs=[vmem, pl.BlockSpec(memory_space=pl.ANY)] + [vmem] * 5
        + [pl.BlockSpec(memory_space=pltpu.SMEM), vmem],
        out_specs=vmem,
        scratch_shapes=[
            pltpu.VMEM((taps * phases * voxels, 2 * voxels), bf16),
            pltpu.VMEM((owners, contrib), f32),
            pltpu.VMEM((owners * INFO, contrib), bf16),
            pltpu.VMEM((owners * INFO, wide), f32),
            pltpu.VMEM((bundle * cap, taps * phases * voxels), bf16),
            pltpu.VMEM((tile_rows, 2 * voxels), f32),
            pltpu.VMEM((2, nodes), f32),
            pltpu.VMEM((plane, 2, nodes), f32),
            pltpu.VMEM((owners, cap + META, voxels), bf16),
            pltpu.VMEM((owners, cap + META, voxels), bf16),
            pltpu.SemaphoreType.DMA,
            pltpu.SemaphoreType.DMA((plane,)),
            pltpu.SemaphoreType.DMA((plane,)),
            pltpu.SemaphoreType.DMA((owners,)),
            pltpu.SemaphoreType.DMA((owners,)),
        ],
        compiler_params=pltpu.CompilerParams(
            collective_id=0, has_side_effects=True, vmem_limit_bytes=56 * 1024 * 1024
        ),
    )(
        source_rows,
        interp_bank.reshape(taps * phases * voxels, 2 * voxels),
        source_taps,
        tap_phase,
        mesh_node.reshape(1, contrib),
        target_tile.reshape(1, contrib),
        target_row.reshape(1, contrib),
        tile_owner,
        coarse_mesh,
    )


def solution(mesh):
    return jax.shard_map(
        on_device,
        mesh=mesh,
        in_specs=(
            P(("slab", "xy", "gz"), None),
            P(),
            P(None, ("slab", "xy", "gz")),
            P(None, ("slab", "xy", "gz")),
            P(("slab", "xy", "gz")),
            P(("slab", "xy", "gz"), None),
            P(("slab", "xy", "gz")),
            P("slab"),
            P(("slab", "gz"), None, "xy"),
        ),
        out_specs=P(("slab", "xy", "gz"), None),
        check_vma=False,
    )
```

```python
import functools

import jax
import jax.numpy as jnp
from jax import lax
from jax.experimental import pallas as pl
from jax.experimental.pallas import tpu as pltpu
from jax.sharding import PartitionSpec as P

floor_weight = 0.1
LANES = 128
INFO = 16
MESH_ROW = 6
META = 16
f32, bf16, i32 = jnp.float32, jnp.bfloat16, jnp.int32
NT = (((1,), (1,)), ((), ()))


def flip(a, b, count):
    out, bit = 0, 1
    while bit < count:
        out = out + ((a // bit + b // bit) % 2) * bit
        bit *= 2
    return out


def flip_static(a, b, count):
    out, bit = a, 1
    while bit < count:
        if (b // bit) % 2:
            out = out + bit - 2 * bit * ((a // bit) % 2)
        bit *= 2
    return out


def one_hot(columns, values):
    return jnp.where(columns == values, 1.0, 0.0).astype(bf16)


def kernel(
    sizes,
    source_ref, bank_hbm, taps_ref, phase_ref, node_ref, tile_ref, row_ref, owner_ref, mesh_ref,
    out_ref,
    spread_src, bank, member, info_rows, info_all, placed, acc, mesh_own, mesh_got, sent, got,
    bank_sem, mesh_send, mesh_recv, send_sem, recv_sem,
):
    contrib, owners, plane, group, cap, wide, nodes = sizes
    voxels = source_ref.shape[1]
    parts_src = source_ref.shape[0] // 256
    tile_rows = out_ref.shape[0]
    phases = placed.shape[1] // (2 * voxels)
    spread = float(voxels // 4)
    slab_at, xy_at, gz_at = lax.axis_index("slab"), lax.axis_index("xy"), lax.axis_index("gz")
    me = xy_at * group + gz_at

    def device(step):
        other = flip(me, step, owners)
        return (slab_at, other // group, other % group)

    barrier = pltpu.get_barrier_semaphore()

    for step in range(1, owners):
        other = flip_static(me, step, owners)
        there = (slab_at, other // group, other % group)
        pl.semaphore_signal(barrier, inc=1, device_id=there, device_id_type=pl.DeviceIdType.MESH)

    bank_copy = pltpu.make_async_copy(bank_hbm, bank, bank_sem)
    bank_copy.start()

    part = mesh_ref.shape[2]
    place = jnp.where(
        lax.broadcasted_iota(i32, (part, nodes), 1) == lax.broadcasted_iota(i32, (part, nodes), 0) + xy_at * part, 1.0, 0.0
    )
    mesh_own[...] = jnp.dot(mesh_ref[0], place, precision=lax.Precision.HIGHEST, preferred_element_type=f32)

    tiles = tile_ref[...]
    owner = jnp.zeros_like(tiles)
    for tile in range(owners):
        owner = jnp.where(tiles == tile, owner_ref[tile], owner)
    relative = jnp.bitwise_xor(owner, me)
    chosen = jnp.where(lax.broadcasted_iota(i32, (owners, contrib), 0) == relative, 1.0, 0.0)
    member[...] = chosen
    chunk = 256
    before = (
        lax.broadcasted_iota(i32, (chunk, chunk), 0) < lax.broadcasted_iota(i32, (chunk, chunk), 1)
    ).astype(f32).astype(bf16)
    carry = jnp.zeros((owners, 1), f32)
    ranks = []
    for at in range(0, contrib, chunk):
        here = chosen[:, at : at + chunk]
        earlier = jnp.dot(here.astype(bf16), before, preferred_element_type=f32) + carry
        ranks.append(jnp.sum(here * earlier, axis=0, keepdims=True))
        carry = carry + jnp.sum(here, axis=1, keepdims=True)
    rank = jnp.concatenate(ranks, axis=1)
    pl.semaphore_wait(barrier, owners - 1)

    def mesh_copy(step):
        return pltpu.make_async_remote_copy(
            src_ref=mesh_own,
            dst_ref=mesh_got.at[step],
            send_sem=mesh_send.at[step],
            recv_sem=mesh_recv.at[step],
            device_id=(slab_at, flip_static(xy_at, step, plane), gz_at),
            device_id_type=pl.DeviceIdType.MESH,
        )

    for step in range(1, plane):
        mesh_copy(step).start()

    rank_hot = one_hot(lax.broadcasted_iota(i32, (wide, contrib), 0).astype(f32), rank)
    node_hot = one_hot(lax.broadcasted_iota(i32, (nodes, contrib), 0), node_ref[...])

    for step in range(1, plane):
        mesh_copy(step).wait_recv()

    mesh = mesh_own[...]
    for step in range(1, plane):
        mesh = mesh + mesh_got[step]
    shift, center = mesh[0:1], (voxels - 1) * mesh[1:2]
    high = shift.astype(bf16).astype(f32)
    middle = (shift - high).astype(bf16).astype(f32)
    low = shift - high - middle
    spot = lax.broadcasted_iota(i32, (INFO, nodes), 0)
    table = jnp.zeros((INFO, nodes), f32)
    for at, line in enumerate((high, middle, low, center)):
        table = jnp.where(spot == MESH_ROW + at, line, table)
    info = jnp.dot(table.astype(bf16), node_hot, preferred_element_type=f32)
    target = row_ref[...] + 1
    taps0, taps1 = taps_ref[0:1, :], taps_ref[1:2, :]
    lines = {
        0: taps0 // 256, 1: taps0 % 256, 2: taps1 // 256, 3: taps1 % 256,
        4: phase_ref[0:1, :], 5: phase_ref[1:2, :],
        10: target // 256, 11: target % 256,
    }
    spot = lax.broadcasted_iota(i32, (INFO, contrib), 0)
    for at, line in lines.items():
        info = jnp.where(spot == at, line.astype(f32), info)

    @pl.loop(0, owners)
    def _(step):
        info_rows[pl.ds(pl.multiple_of(step * INFO, INFO), INFO), :] = (
            info * member[pl.ds(step, 1), :]
        ).astype(bf16)

    for at in range(parts_src):
        spread_src[:, at * voxels : (at + 1) * voxels] = source_ref[at * 256 : (at + 1) * 256, :]
    info_all[...] = lax.dot_general(info_rows[...], rank_hot, NT, preferred_element_type=f32)
    acc[...] = jnp.zeros_like(acc)
    bank_copy.wait()

    def value_copy(step):
        return pltpu.make_async_remote_copy(
            src_ref=sent.at[step],
            dst_ref=got.at[step],
            send_sem=send_sem.at[step],
            recv_sem=recv_sem.at[step],
            device_id=device(step),
            device_id_type=pl.DeviceIdType.MESH,
        )

    bundle = max(1, 512 // cap)
    size = bundle * cap
    lines_each = wide // LANES

    def produce(first):
        pieces = []
        for d in range(bundle):
            lanes = info_all[pl.ds(pl.multiple_of((first + d) * INFO, INFO), INFO), :]
            pieces.append(lanes.T[:cap])
            meta = [lanes[r : r + 1, at * LANES : (at + 1) * LANES] for r in (9, 10, 11) for at in range(lines_each)]
            spot = lax.broadcasted_iota(i32, (META, LANES), 0)
            filled = jnp.zeros((META, LANES), f32)
            for at, line in enumerate(meta):
                filled = jnp.where(spot == at, line, filled)
            sent[first + d, cap : cap + META, :] = filled.astype(bf16)
        columns = pieces[0] if bundle == 1 else jnp.concatenate(pieces, axis=0)
        ids = lax.broadcasted_iota(i32, (size, 256), 1).astype(f32)
        hot = jnp.concatenate([one_hot(ids, columns[:, 1:2]), one_hot(ids, columns[:, 3:4])], axis=0)
        quads = jnp.dot(hot, spread_src[...], preferred_element_type=f32).astype(bf16)
        for k in range(2):
            quad = quads[k * size : (k + 1) * size]
            high = jnp.broadcast_to(columns[:, 2 * k : 2 * k + 1], (size, voxels)).astype(bf16)
            picked = quad[:, :voxels]
            for at in range(1, parts_src):
                picked = jnp.where(high == jnp.bfloat16(at), quad[:, at * voxels : (at + 1) * voxels], picked)
            phase = jnp.broadcast_to(columns[:, 4 + k : 5 + k], (size, voxels)).astype(bf16)
            for p in range(phases):
                at = (k * phases + p) * voxels
                placed[:, at : at + voxels] = jnp.where(phase == jnp.bfloat16(p), picked, jnp.bfloat16(0))
        products = jnp.dot(placed[...], bank[...], preferred_element_type=f32)
        weight = columns[:, MESH_ROW : MESH_ROW + 1] + columns[:, MESH_ROW + 1 : MESH_ROW + 2]
        weight = weight + columns[:, MESH_ROW + 2 : MESH_ROW + 3]
        mixed = ((1.0 - weight) * products[:, :voxels] + weight * products[:, voxels:]).astype(bf16)
        for d in range(bundle):
            sent[first + d, :cap, :] = mixed[d * cap : (d + 1) * cap]

            @pl.when(first + d > 0)
            def _():
                value_copy(first + d).start()

            @pl.when(first + d == 0)
            def _():
                got[0] = sent[0]

    def consume(first):
        targets, operands = [], []
        for d in range(bundle):
            step = first + d

            @pl.when(step > 0)
            def _():
                value_copy(step).wait_recv()

            meta = got[step, cap : cap + META, :].astype(f32)
            target = meta[lines_each : 2 * lines_each] * 256.0 + meta[2 * lines_each : 3 * lines_each]
            targets.append(jnp.concatenate([target[at : at + 1] for at in range(lines_each)], axis=1)[:, :cap])
            turned = meta.T
            center = jnp.concatenate([turned[:, at : at + 1] for at in range(lines_each)], axis=0)[:cap]
            offsets = lax.broadcasted_iota(i32, (cap, voxels), 1).astype(f32) - center
            weights = jnp.exp(-0.5 * (offsets / spread) ** 2)
            values = got[step, :cap, :].astype(f32)
            operands.append(jnp.concatenate([weights * values, weights], axis=1).astype(bf16))
        ids = lax.broadcasted_iota(i32, (tile_rows, cap), 0).astype(f32) + 1.0
        hot = jnp.concatenate([one_hot(ids, target) for target in targets], axis=1)
        acc[...] += jnp.dot(hot, jnp.concatenate(operands, axis=0), preferred_element_type=f32)

    blocks = owners // bundle

    @pl.loop(0, blocks)
    def _(turn):
        produce((blocks - 1 - turn) * bundle)

    @pl.loop(0, blocks)
    def _(turn):
        half = blocks // 2
        consume(jnp.where(turn < half, turn, blocks - 1 - turn + half) * bundle)

    out_ref[...] = (acc[:, :voxels] / jnp.maximum(acc[:, voxels:], floor_weight)).astype(bf16)

    for step in range(1, plane):
        mesh_copy(step).wait_send()

    @pl.loop(1, owners)
    def _(step):
        value_copy(step).wait_send()


def on_device(
    source_rows,
    interp_bank,
    source_taps,
    tap_phase,
    mesh_node,
    target_tile,
    target_row,
    tile_owner,
    coarse_mesh,
):
    contrib = mesh_node.shape[0]
    voxels = source_rows.shape[1]
    taps, phases = interp_bank.shape[:2]
    plane = lax.axis_size("xy")
    group = lax.axis_size("gz")
    owners = plane * group
    cap = 2 * contrib // owners
    wide = max(cap, LANES)
    tile_rows = contrib // 2
    nodes = plane * coarse_mesh.shape[2]
    bundle = max(1, 512 // cap)
    vmem = pl.BlockSpec(memory_space=pltpu.VMEM)
    return pl.pallas_call(
        functools.partial(kernel, (contrib, owners, plane, group, cap, wide, nodes)),
        out_shape=jax.ShapeDtypeStruct((tile_rows, voxels), bf16),
        in_specs=[vmem, pl.BlockSpec(memory_space=pl.ANY)] + [vmem] * 5
        + [pl.BlockSpec(memory_space=pltpu.SMEM), vmem],
        out_specs=vmem,
        scratch_shapes=[
            pltpu.VMEM((256, source_rows.shape[0] // 256 * voxels), bf16),
            pltpu.VMEM((taps * phases * voxels, 2 * voxels), bf16),
            pltpu.VMEM((owners, contrib), f32),
            pltpu.VMEM((owners * INFO, contrib), bf16),
            pltpu.VMEM((owners * INFO, wide), f32),
            pltpu.VMEM((bundle * cap, taps * phases * voxels), bf16),
            pltpu.VMEM((tile_rows, 2 * voxels), f32),
            pltpu.VMEM((2, nodes), f32),
            pltpu.VMEM((plane, 2, nodes), f32),
            pltpu.VMEM((owners, cap + META, voxels), bf16),
            pltpu.VMEM((owners, cap + META, voxels), bf16),
            pltpu.SemaphoreType.DMA,
            pltpu.SemaphoreType.DMA((plane,)),
            pltpu.SemaphoreType.DMA((plane,)),
            pltpu.SemaphoreType.DMA((owners,)),
            pltpu.SemaphoreType.DMA((owners,)),
        ],
        compiler_params=pltpu.CompilerParams(
            collective_id=0, has_side_effects=True, vmem_limit_bytes=56 * 1024 * 1024
        ),
    )(
        source_rows,
        interp_bank.reshape(taps * phases * voxels, 2 * voxels),
        source_taps,
        tap_phase,
        mesh_node.reshape(1, contrib),
        target_tile.reshape(1, contrib),
        target_row.reshape(1, contrib),
        tile_owner,
        coarse_mesh,
    )


def solution(mesh):
    return jax.shard_map(
        on_device,
        mesh=mesh,
        in_specs=(
            P(("slab", "xy", "gz"), None),
            P(),
            P(None, ("slab", "xy", "gz")),
            P(None, ("slab", "xy", "gz")),
            P(("slab", "xy", "gz")),
            P(("slab", "xy", "gz"), None),
            P(("slab", "xy", "gz")),
            P("slab"),
            P(("slab", "gz"), None, "xy"),
        ),
        out_specs=P(("slab", "xy", "gz"), None),
        check_vma=False,
    )
```

```python
import functools

import jax
import jax.numpy as jnp
from jax import lax
from jax.experimental import pallas as pl
from jax.experimental.pallas import tpu as pltpu
from jax.sharding import PartitionSpec as P

floor_weight = 0.1
LANES = 128
INFO = 16
MESH_ROW = 6
f32, bf16, i32 = jnp.float32, jnp.bfloat16, jnp.int32
NT = (((1,), (1,)), ((), ()))


def flip(a, b, count):
    out, bit = 0, 1
    while bit < count:
        out = out + ((a // bit + b // bit) % 2) * bit
        bit *= 2
    return out


def flip_static(a, b, count):
    out, bit = a, 1
    while bit < count:
        if (b // bit) % 2:
            out = out + bit - 2 * bit * ((a // bit) % 2)
        bit *= 2
    return out


def one_hot(columns, values):
    return jnp.where(columns == values, 1.0, 0.0).astype(bf16)


def kernel(
    sizes,
    source_ref, bank_hbm, taps_ref, phase_ref, node_ref, tile_ref, row_ref, owner_ref, mesh_ref,
    out_ref,
    spread_src, bank, member, info_rows, info_all, info_turned, placed, acc, mesh_own, mesh_got, sent, got, notes_sent, notes_got,
    bank_sem, mesh_send, mesh_recv, send_sem, recv_sem, note_send, note_recv,
):
    contrib, owners, plane, group, cap, wide, nodes = sizes
    voxels = source_ref.shape[1]
    parts_src = source_ref.shape[0] // 256
    tile_rows = out_ref.shape[0]
    phases = placed.shape[1] // (2 * voxels)
    spread = float(voxels // 4)
    slab_at, xy_at, gz_at = lax.axis_index("slab"), lax.axis_index("xy"), lax.axis_index("gz")
    me = xy_at * group + gz_at

    def device(step):
        other = flip(me, step, owners)
        return (slab_at, other // group, other % group)

    barrier = pltpu.get_barrier_semaphore()

    for step in range(1, owners):
        other = flip_static(me, step, owners)
        there = (slab_at, other // group, other % group)
        pl.semaphore_signal(barrier, inc=1, device_id=there, device_id_type=pl.DeviceIdType.MESH)

    bank_copy = pltpu.make_async_copy(bank_hbm, bank, bank_sem)
    bank_copy.start()

    part = mesh_ref.shape[2]
    place = jnp.where(
        lax.broadcasted_iota(i32, (part, nodes), 1) == lax.broadcasted_iota(i32, (part, nodes), 0) + xy_at * part, 1.0, 0.0
    )
    mesh_own[...] = jnp.dot(mesh_ref[0], place, precision=lax.Precision.HIGHEST, preferred_element_type=f32)

    tiles = tile_ref[...]
    owner = jnp.zeros_like(tiles)
    for tile in range(owners):
        owner = jnp.where(tiles == tile, owner_ref[tile], owner)
    relative = jnp.bitwise_xor(owner, me)
    chosen = jnp.where(lax.broadcasted_iota(i32, (owners, contrib), 0) == relative, 1.0, 0.0)
    member[...] = chosen
    chunk = 256
    before = (
        lax.broadcasted_iota(i32, (chunk, chunk), 0) < lax.broadcasted_iota(i32, (chunk, chunk), 1)
    ).astype(f32).astype(bf16)
    carry = jnp.zeros((owners, 1), f32)
    ranks = []
    for at in range(0, contrib, chunk):
        here = chosen[:, at : at + chunk]
        earlier = jnp.dot(here.astype(bf16), before, preferred_element_type=f32) + carry
        ranks.append(jnp.sum(here * earlier, axis=0, keepdims=True))
        carry = carry + jnp.sum(here, axis=1, keepdims=True)
    rank = jnp.concatenate(ranks, axis=1)
    pl.semaphore_wait(barrier, owners - 1)

    def mesh_copy(step):
        return pltpu.make_async_remote_copy(
            src_ref=mesh_own,
            dst_ref=mesh_got.at[step],
            send_sem=mesh_send.at[step],
            recv_sem=mesh_recv.at[step],
            device_id=(slab_at, flip_static(xy_at, step, plane), gz_at),
            device_id_type=pl.DeviceIdType.MESH,
        )

    for step in range(1, plane):
        mesh_copy(step).start()

    rank_hot = one_hot(lax.broadcasted_iota(i32, (wide, contrib), 0).astype(f32), rank)
    node_hot = one_hot(lax.broadcasted_iota(i32, (nodes, contrib), 0), node_ref[...])

    for step in range(1, plane):
        mesh_copy(step).wait_recv()

    mesh = mesh_own[...]
    for step in range(1, plane):
        mesh = mesh + mesh_got[step]
    shift, center = mesh[0:1], (voxels - 1) * mesh[1:2]
    high = shift.astype(bf16).astype(f32)
    middle = (shift - high).astype(bf16).astype(f32)
    low = shift - high - middle
    spot = lax.broadcasted_iota(i32, (INFO, nodes), 0)
    table = jnp.zeros((INFO, nodes), f32)
    for at, line in enumerate((high, middle, low, center)):
        table = jnp.where(spot == MESH_ROW + at, line, table)
    info = jnp.dot(table.astype(bf16), node_hot, preferred_element_type=f32)
    target = row_ref[...] + 1
    taps0, taps1 = taps_ref[0:1, :], taps_ref[1:2, :]
    lines = {
        0: taps0 // 256, 1: taps0 % 256, 2: taps1 // 256, 3: taps1 % 256,
        4: phase_ref[0:1, :], 5: phase_ref[1:2, :],
        10: target // 256, 11: target % 256,
    }
    spot = lax.broadcasted_iota(i32, (INFO, contrib), 0)
    for at, line in lines.items():
        info = jnp.where(spot == at, line.astype(f32), info)

    @pl.loop(0, owners)
    def _(step):
        info_rows[pl.ds(pl.multiple_of(step * INFO, INFO), INFO), :] = (
            info * member[pl.ds(step, 1), :]
        ).astype(bf16)

    for at in range(parts_src):
        spread_src[:, at * voxels : (at + 1) * voxels] = source_ref[at * 256 : (at + 1) * 256, :]
    info_all[...] = lax.dot_general(info_rows[...], rank_hot, NT, preferred_element_type=f32)
    info_turned[...] = info_all[...].T
    acc[...] = jnp.zeros_like(acc)
    bank_copy.wait()

    def value_copy(step):
        return pltpu.make_async_remote_copy(
            src_ref=sent.at[step],
            dst_ref=got.at[step],
            send_sem=send_sem.at[step],
            recv_sem=recv_sem.at[step],
            device_id=device(step),
            device_id_type=pl.DeviceIdType.MESH,
        )

    def note_copy(step):
        return pltpu.make_async_remote_copy(
            src_ref=notes_sent.at[step],
            dst_ref=notes_got.at[step],
            send_sem=note_send.at[step],
            recv_sem=note_recv.at[step],
            device_id=device(step),
            device_id_type=pl.DeviceIdType.MESH,
        )

    bundle = max(1, 512 // cap)
    size = bundle * cap
    lines_each = wide // LANES

    def produce(first):
        pieces = []
        for d in range(bundle):
            lanes = info_all[pl.ds(pl.multiple_of((first + d) * INFO, INFO), INFO), :]
            width = owners * INFO
            pieces.append(pltpu.roll(info_turned[:cap, :], (width - (first + d) * INFO) % width, 1))
            center, target = lanes[9:10], lanes[10:11] * 256.0 + lanes[11:12]
            for at in range(lines_each):
                notes_sent[first + d, at : at + 1, :] = center[:, at * LANES : (at + 1) * LANES]
                notes_sent[first + d, lines_each + at : lines_each + at + 1, :] = target[:, at * LANES : (at + 1) * LANES]
        columns = pieces[0] if bundle == 1 else jnp.concatenate(pieces, axis=0)
        ids = lax.broadcasted_iota(i32, (size, 256), 1).astype(f32)
        hot = jnp.concatenate([one_hot(ids, columns[:, 1:2]), one_hot(ids, columns[:, 3:4])], axis=0)
        quads = jnp.dot(hot, spread_src[...], preferred_element_type=f32).astype(bf16)
        for k in range(2):
            quad = quads[k * size : (k + 1) * size]
            high = jnp.broadcast_to(columns[:, 2 * k : 2 * k + 1], (size, voxels)).astype(bf16)
            picked = quad[:, :voxels]
            for at in range(1, parts_src):
                picked = jnp.where(high == jnp.bfloat16(at), quad[:, at * voxels : (at + 1) * voxels], picked)
            phase = jnp.broadcast_to(columns[:, 4 + k : 5 + k], (size, voxels)).astype(bf16)
            for p in range(phases):
                at = (k * phases + p) * voxels
                placed[:, at : at + voxels] = jnp.where(phase == jnp.bfloat16(p), picked, jnp.bfloat16(0))
        products = jnp.dot(placed[...], bank[...], preferred_element_type=f32)
        weight = columns[:, MESH_ROW : MESH_ROW + 1] + columns[:, MESH_ROW + 1 : MESH_ROW + 2]
        weight = weight + columns[:, MESH_ROW + 2 : MESH_ROW + 3]
        mixed = ((1.0 - weight) * products[:, :voxels] + weight * products[:, voxels:]).astype(bf16)
        for d in range(bundle):
            sent[first + d, :cap, :] = mixed[d * cap : (d + 1) * cap]

            @pl.when(first + d > 0)
            def _():
                note_copy(first + d).start()
                value_copy(first + d).start()

            @pl.when(first + d == 0)
            def _():
                got[0] = sent[0]
                notes_got[0] = notes_sent[0]

    def consume(first):
        targets, operands = [], []
        for d in range(bundle):
            step = first + d

            @pl.when(step > 0)
            def _():
                note_copy(step).wait_recv()
                value_copy(step).wait_recv()

            notes = notes_got[step]
            target = notes[lines_each:]
            targets.append(jnp.concatenate([target[at : at + 1] for at in range(lines_each)], axis=1)[:, :cap])
            turned = notes.T
            center = jnp.concatenate([turned[:, at : at + 1] for at in range(lines_each)], axis=0)[:cap]
            offsets = lax.broadcasted_iota(i32, (cap, voxels), 1).astype(f32) - center
            weights = jnp.exp(-0.5 * (offsets / spread) ** 2)
            values = got[step, :cap, :].astype(f32)
            operands.append(jnp.concatenate([weights * values, weights], axis=1).astype(bf16))
        ids = lax.broadcasted_iota(i32, (tile_rows, cap), 0).astype(f32) + 1.0
        hot = jnp.concatenate([one_hot(ids, target) for target in targets], axis=1)
        acc[...] += jnp.dot(hot, jnp.concatenate(operands, axis=0), preferred_element_type=f32)

    blocks = owners // bundle

    @pl.loop(0, blocks)
    def _(turn):
        produce((blocks - 1 - turn // 2 - blocks // 2 * (turn % 2)) * bundle)

    @pl.loop(0, blocks)
    def _(turn):
        half = blocks // 2
        consume(jnp.where(turn < half, turn, blocks - 1 - turn + half) * bundle)

    out_ref[...] = (acc[:, :voxels] / jnp.maximum(acc[:, voxels:], floor_weight)).astype(bf16)

    for step in range(1, plane):
        mesh_copy(step).wait_send()

    @pl.loop(1, owners)
    def _(step):
        note_copy(step).wait_send()
        value_copy(step).wait_send()


def on_device(
    source_rows,
    interp_bank,
    source_taps,
    tap_phase,
    mesh_node,
    target_tile,
    target_row,
    tile_owner,
    coarse_mesh,
):
    contrib = mesh_node.shape[0]
    voxels = source_rows.shape[1]
    taps, phases = interp_bank.shape[:2]
    plane = lax.axis_size("xy")
    group = lax.axis_size("gz")
    owners = plane * group
    cap = 2 * contrib // owners
    wide = max(cap, LANES)
    tile_rows = contrib // 2
    nodes = plane * coarse_mesh.shape[2]
    bundle = max(1, 512 // cap)
    vmem = pl.BlockSpec(memory_space=pltpu.VMEM)
    return pl.pallas_call(
        functools.partial(kernel, (contrib, owners, plane, group, cap, wide, nodes)),
        out_shape=jax.ShapeDtypeStruct((tile_rows, voxels), bf16),
        in_specs=[vmem, pl.BlockSpec(memory_space=pl.ANY)] + [vmem] * 5
        + [pl.BlockSpec(memory_space=pltpu.SMEM), vmem],
        out_specs=vmem,
        scratch_shapes=[
            pltpu.VMEM((256, source_rows.shape[0] // 256 * voxels), bf16),
            pltpu.VMEM((taps * phases * voxels, 2 * voxels), bf16),
            pltpu.VMEM((owners, contrib), f32),
            pltpu.VMEM((owners * INFO, contrib), bf16),
            pltpu.VMEM((owners * INFO, wide), f32),
            pltpu.VMEM((wide, owners * INFO), f32),
            pltpu.VMEM((bundle * cap, taps * phases * voxels), bf16),
            pltpu.VMEM((tile_rows, 2 * voxels), f32),
            pltpu.VMEM((2, nodes), f32),
            pltpu.VMEM((plane, 2, nodes), f32),
            pltpu.VMEM((owners, cap, voxels), bf16),
            pltpu.VMEM((owners, cap, voxels), bf16),
            pltpu.VMEM((owners, 2 * wide // LANES, LANES), f32),
            pltpu.VMEM((owners, 2 * wide // LANES, LANES), f32),
            pltpu.SemaphoreType.DMA,
            pltpu.SemaphoreType.DMA((plane,)),
            pltpu.SemaphoreType.DMA((plane,)),
            pltpu.SemaphoreType.DMA((owners,)),
            pltpu.SemaphoreType.DMA((owners,)),
            pltpu.SemaphoreType.DMA((owners,)),
            pltpu.SemaphoreType.DMA((owners,)),
        ],
        compiler_params=pltpu.CompilerParams(
            collective_id=0, has_side_effects=True, vmem_limit_bytes=56 * 1024 * 1024
        ),
    )(
        source_rows,
        interp_bank.reshape(taps * phases * voxels, 2 * voxels),
        source_taps,
        tap_phase,
        mesh_node.reshape(1, contrib),
        target_tile.reshape(1, contrib),
        target_row.reshape(1, contrib),
        tile_owner,
        coarse_mesh,
    )


def solution(mesh):
    return jax.shard_map(
        on_device,
        mesh=mesh,
        in_specs=(
            P(("slab", "xy", "gz"), None),
            P(),
            P(None, ("slab", "xy", "gz")),
            P(None, ("slab", "xy", "gz")),
            P(("slab", "xy", "gz")),
            P(("slab", "xy", "gz"), None),
            P(("slab", "xy", "gz")),
            P("slab"),
            P(("slab", "gz"), None, "xy"),
        ),
        out_specs=P(("slab", "xy", "gz"), None),
        check_vma=False,
    )
```
